1024 devices in a mesh: fsdp: 64 (over z_hi, x, core), tp: 16 (over z_lo, y).
Axes of the slice: x: 8, y: 8, z: 8 (z_hi: 4, z_lo: 2; z = z_hi * 2 + z_lo), core: 2. Of those that a mesh axis runs over, the one named last changes fastest.
Arguments:
- tokens: bfloat16 [1024, 16384], P('tp', 'fsdp'), may hold values from -16 to 16
- out_grad: bfloat16 [1024, 16384], P('tp', 'fsdp'), may hold values from -16 to 16
- gate_rows: bfloat16 [8192, 16384], P('tp', 'fsdp'), may hold values from -0.046875 to 0.046875
- up_rows: bfloat16 [8192, 16384], P('tp', 'fsdp'), may hold values from -0.046875 to 0.046875
- down_rows: bfloat16 [8192, 16384], P('tp', 'fsdp'), may hold values from -0.046875 to 0.046875
Outputs:
- input_grad: bfloat16 [1024, 16384], P('tp', 'fsdp')
- gate_grad: float32 [8192, 16384], P('tp', 'fsdp')
- up_grad: float32 [8192, 16384], P('tp', 'fsdp')
- down_grad: float32 [8192, 16384], P('tp', 'fsdp')
The draws below stay inside these ranges and needn't reach their ends.
All inputs are finite; a program needn't handle non-finite values.
Results may differ from the reference program's by a relative error of at most 0.023.
Values may be sent and summed in bfloat16 or wider, within the bound.
No kernel may reach another device: no remote copies, remote signals or barrier semaphores. Data moves between devices by JAX's collectives and lax.ppermute only.
A program may use at most 32 MiB of HBM per device.

```python
import jax
import jax.numpy as jnp
from jax import lax

D = 16384
FF = 8192
TOKENS = 1024
N_TP = 16


def strengthened(drawn, key, source, target, shards_of, factor):
    owner, partner = [(jnp.arange(drawn.shape[position]) // (drawn.shape[position] // shards_of)).reshape([-1 if axis == position else 1 for axis in range(drawn.ndim)]) for position in (source, target)]
    chosen = jax.random.permutation(key, shards_of)[partner]
    strong = (owner == chosen) | (owner == (partner + shards_of // 2) % shards_of)
    return jnp.where(strong, factor * drawn, drawn)


def shard_levels(key, shape, cuts, low, largest):
    def one(axis_at, parts):
        steps = jax.random.uniform(jax.random.fold_in(jax.random.fold_in(key, 6), axis_at), (parts,), jnp.float32, low / len(cuts), largest / len(cuts))
        return jnp.repeat(jnp.exp(steps), shape[axis_at] // parts).reshape((-1,) + (1,) * (len(shape) - axis_at - 1))

    level = one(*cuts[0])
    for cut in cuts[1:]:
        level = level * one(*cut)
    return level


def noise(own_key, shape, scale, bound, pieces=(), kind=jnp.bfloat16):
    result = jax.random.normal(own_key, shape, jnp.float32) * scale
    if len(pieces) > 0:
        result = shard_levels(own_key, shape, pieces, -0.22, 0.18) * result
    return jnp.clip(result, min=-bound, max=bound).astype(kind)


def bell_draw_with(rng, shape, deviation, most, split, heavy, kind=jnp.bfloat16):
    values = deviation * jax.random.normal(rng, shape, jnp.float32)
    if split:
        values = values * shard_levels(rng, shape, split, -0.22, 0.18)
    return jnp.clip(strengthened(values, jax.random.fold_in(rng, 3), *heavy), -most, most).astype(kind)


def setup_inputs(seed: int = 0) -> dict:
    keys = jax.random.split(jax.random.key(seed), 6)
    return {
        "tokens": bell_draw_with(keys[0], (TOKENS, D), 1.0, 16.0, ((0, 16), (1, 64)), (1, 0, 64, 4.0)),
        "out_grad": bell_draw_with(keys[1], (TOKENS, D), 1.0, 16.0, ((0, 16), (1, 64)), (1, 0, 64, 4.0)),
        "gate_rows": noise(keys[2], (FF, D), D ** -0.5, 0.046875, ((0, 16), (1, 64))),
        "up_rows": noise(keys[3], (FF, D), D ** -0.5, 0.046875, ((0, 16), (1, 64))),
        "down_rows": noise(keys[4], (FF, D), D ** -0.5, 0.046875, ((0, 16), (1, 64))),
    }


def reference(tokens, out_grad, gate_rows, up_rows, down_rows):
    dims = (((1,), (1,)), ((), ()))
    gate = lax.dot_general(tokens, gate_rows, dims, preferred_element_type=jnp.float32)
    up = lax.dot_general(tokens, up_rows, dims, preferred_element_type=jnp.float32)
    sig = 1.0 / (1.0 + jnp.exp(-gate))
    hidden = (gate * sig * up).astype(jnp.bfloat16)
    hidden_grad = lax.dot_general(out_grad, down_rows, dims, preferred_element_type=jnp.float32)
    gate_pre = (hidden_grad * up * sig * (1.0 + gate * (1.0 - sig))).astype(jnp.bfloat16)
    up_pre = (hidden_grad * gate * sig).astype(jnp.bfloat16)
    width = FF // N_TP

    def block_step(total, index):
        start = (index * width).astype(jnp.int32)
        gate_part = lax.dynamic_slice_in_dim(gate_pre, start, width, 1)
        up_part = lax.dynamic_slice_in_dim(up_pre, start, width, 1)
        gate_block = lax.dynamic_slice_in_dim(gate_rows, start, width, 0)
        up_block = lax.dynamic_slice_in_dim(up_rows, start, width, 0)
        part = jnp.dot(gate_part, gate_block, preferred_element_type=jnp.float32)
        part = part + jnp.dot(up_part, up_block, preferred_element_type=jnp.float32)
        return total + part.astype(jnp.bfloat16).astype(jnp.float32), None

    start_total = jnp.zeros((tokens.shape[0], tokens.shape[1]), jnp.float32)
    total, _ = lax.scan(block_step, start_total, jnp.arange(N_TP, dtype=jnp.int32))
    input_grad = total.astype(jnp.bfloat16)
    tdims = (((0,), (0,)), ((), ()))
    gate_grad = lax.dot_general(gate_pre, tokens, tdims, preferred_element_type=jnp.float32)
    up_grad = lax.dot_general(up_pre, tokens, tdims, preferred_element_type=jnp.float32)
    down_grad = lax.dot_general(hidden, out_grad, tdims, preferred_element_type=jnp.float32)
    return (input_grad, gate_grad, up_grad, down_grad)
```

```python
import jax
import jax.numpy as jnp
from jax import lax
from jax.sharding import PartitionSpec as P

Z_HI, CORES = 4, 2


def activate(gate, up, hidden_grad):
    sig = 1.0 / (1.0 + jnp.exp(-gate))
    hidden = (gate * sig * up).astype(jnp.bfloat16)
    gate_pre = (hidden_grad * up * sig * (1.0 + gate * (1.0 - sig))).astype(jnp.bfloat16)
    up_pre = (hidden_grad * gate * sig).astype(jnp.bfloat16)
    return (hidden, gate_pre, up_pre)


def swapped(value, axis, pairs):
    return lax.ppermute(value, axis, pairs)


def spread(value, axis, count, groups=None):
    copies = jnp.broadcast_to(value[None], (count,) + value.shape).reshape((-1,) + value.shape[1:])
    return exchange(copies, axis, groups)


def exchange(value, axis, groups=None):
    return lax.all_to_all(value, axis, split_axis=0, concat_axis=0, tiled=True, axis_index_groups=groups)


def solution(mesh):
    n_fsdp, n_tp = mesh.shape["fsdp"], mesh.shape["tp"]
    n_x = n_fsdp // (Z_HI * CORES)
    n_chips = Z_HI * n_x

    def at(z, x, c):
        return (z * n_x + x) * CORES + c

    zs, xs, cs = range(Z_HI), range(n_x), range(CORES)
    core_pairs = [(at(z, x, c), at(z, x, 1 - c)) for z in zs for x in xs for c in cs]
    chip_groups = [[at(z, x, c) for x in xs for z in zs] for c in cs]
    x_groups = [[at(z, x, c) for x in xs] for z in zs for c in cs]
    z_groups = [[at(z, x, c) for z in zs] for x in xs for c in cs]

    def shards(tokens, out_grad, gate_rows, up_rows, down_rows):
        dims = (((1,), (1,)), ((), ()))
        tdims = (((0,), (0,)), ((), ()))
        f32 = jnp.float32
        width = tokens.shape[1]
        half = gate_rows.shape[0] // CORES
        core = lax.axis_index("fsdp") % CORES

        mine = [lax.dynamic_slice_in_dim(w, core * half, half, 0) for w in (gate_rows, up_rows, down_rows)]
        sent = [lax.dynamic_slice_in_dim(w, (1 - core) * half, half, 0) for w in (gate_rows, up_rows, down_rows)]
        got = swapped(jnp.concatenate(sent, axis=0), "fsdp", core_pairs)
        got = [got[i * half : (i + 1) * half] for i in range(3)]

        group = spread(jnp.concatenate([tokens, out_grad], axis=1), "tp", n_tp)
        other = swapped(group, "fsdp", core_pairs)
        x_own, dy_own = group[:, :width], group[:, width:]
        x_oth, dy_oth = other[:, :width], other[:, width:]

        parts = []
        for own, oth, w, v in ((x_own, x_oth, mine[0], got[0]), (x_own, x_oth, mine[1], got[1]), (dy_own, dy_oth, mine[2], got[2])):
            part = lax.dot_general(own, w, dims, preferred_element_type=f32)
            part = part + lax.dot_general(oth, v, dims, preferred_element_type=f32)
            parts.append(part.astype(jnp.bfloat16))
        pieces = exchange(jnp.concatenate(parts, axis=1), "fsdp", chip_groups)
        sums = jnp.sum(pieces.reshape(n_chips, -1, 3 * half).astype(f32), axis=0)
        done = activate(sums[:, :half], sums[:, half : 2 * half], sums[:, 2 * half :])
        done = jnp.concatenate(done, axis=1)

        done = spread(done, "fsdp", Z_HI, z_groups)
        done = lax.all_gather(done, "fsdp", axis=0, tiled=True, axis_index_groups=x_groups)
        back = swapped(done, "fsdp", core_pairs)
        low = jnp.where(core == 0, done, back)
        high = jnp.where(core == 0, back, done)
        hidden, gate_pre, up_pre = [
            jnp.concatenate([low[:, i * half : (i + 1) * half], high[:, i * half : (i + 1) * half]], axis=1)
            for i in range(3)
        ]

        terms = jnp.dot(gate_pre, gate_rows, preferred_element_type=f32)
        terms = terms + jnp.dot(up_pre, up_rows, preferred_element_type=f32)
        terms = exchange(terms.astype(jnp.bfloat16), "tp")
        input_sum = jnp.sum(terms.reshape(n_tp, -1, width).astype(f32), axis=0).astype(jnp.bfloat16)
        gate_grad = lax.dot_general(gate_pre, x_own, tdims, preferred_element_type=f32)
        up_grad = lax.dot_general(up_pre, x_own, tdims, preferred_element_type=f32)
        down_grad = lax.dot_general(hidden, dy_own, tdims, preferred_element_type=f32)
        return (input_sum, gate_grad, up_grad, down_grad)

    spec = P("tp", "fsdp")
    return jax.shard_map(shards, mesh=mesh, in_specs=(spec,) * 5, out_specs=(spec,) * 4, check_vma=False)
```

```python
import jax
import jax.numpy as jnp
from jax import lax
from jax.sharding import PartitionSpec as P

Z_HI, CORES = 4, 2


def activate(gate, up, hidden_grad):
    sig = 1.0 / (1.0 + jnp.exp(-gate))
    hidden = (gate * sig * up).astype(jnp.bfloat16)
    gate_pre = (hidden_grad * up * sig * (1.0 + gate * (1.0 - sig))).astype(jnp.bfloat16)
    up_pre = (hidden_grad * gate * sig).astype(jnp.bfloat16)
    return (hidden, gate_pre, up_pre)


def swapped(value, axis, pairs):
    return lax.ppermute(value, axis, pairs)


def spread(value, axis, count, groups=None):
    copies = jnp.broadcast_to(value[None], (count,) + value.shape).reshape((-1,) + value.shape[1:])
    return exchange(copies, axis, groups)


def exchange(value, axis, groups=None):
    return lax.all_to_all(value, axis, split_axis=0, concat_axis=0, tiled=True, axis_index_groups=groups)


def solution(mesh):
    n_fsdp, n_tp = mesh.shape["fsdp"], mesh.shape["tp"]
    n_x = n_fsdp // (Z_HI * CORES)

    def at(z, x, c):
        return (z * n_x + x) * CORES + c

    zs, xs, cs = range(Z_HI), range(n_x), range(CORES)
    core_pairs = [(at(z, x, c), at(z, x, 1 - c)) for z in zs for x in xs for c in cs]
    far = n_x // 2
    wide_groups = [[at(z, 2 * q + p, 0) for q in range(far)] for z in zs for p in range(2)]
    wide_groups += [[at(z, x, 1) for z in zs] for x in xs]
    near_groups = [[at(z, 2 * q + p, 0) for z in zs for p in range(2)] for q in range(far)]
    near_groups += [[at(z, x, 1) for x in xs] for z in zs]
    n_wide, n_near = len(wide_groups[0]), len(near_groups[0])

    def shards(tokens, out_grad, gate_rows, up_rows, down_rows):
        dims = (((1,), (1,)), ((), ()))
        tdims = (((0,), (0,)), ((), ()))
        f32 = jnp.float32
        width = tokens.shape[1]
        half = gate_rows.shape[0] // CORES
        core = lax.axis_index("fsdp") % CORES

        mine = [lax.dynamic_slice_in_dim(w, core * half, half, 0) for w in (gate_rows, up_rows, down_rows)]
        sent = [lax.dynamic_slice_in_dim(w, (1 - core) * half, half, 0) for w in (gate_rows, up_rows, down_rows)]
        got = swapped(jnp.concatenate(sent, axis=0), "fsdp", core_pairs)
        got = [got[i * half : (i + 1) * half] for i in range(3)]

        group = spread(jnp.concatenate([tokens, out_grad], axis=1), "tp", n_tp)
        other = swapped(group, "fsdp", core_pairs)
        x_own, dy_own = group[:, :width], group[:, width:]
        x_oth, dy_oth = other[:, :width], other[:, width:]

        parts = []
        for own, oth, w, v in ((x_own, x_oth, mine[0], got[0]), (x_own, x_oth, mine[1], got[1]), (dy_own, dy_oth, mine[2], got[2])):
            part = lax.dot_general(own, w, dims, preferred_element_type=f32)
            part = part + lax.dot_general(oth, v, dims, preferred_element_type=f32)
            parts.append(part.astype(jnp.bfloat16))
        pieces = exchange(jnp.concatenate(parts, axis=1), "fsdp", wide_groups)
        sums = jnp.sum(pieces.reshape(n_wide, -1, 3 * half).astype(f32), axis=0).astype(jnp.bfloat16)
        pieces = exchange(sums, "fsdp", near_groups)
        sums = jnp.sum(pieces.reshape(n_near, -1, 3 * half).astype(f32), axis=0)
        done = activate(sums[:, :half], sums[:, half : 2 * half], sums[:, 2 * half :])
        done = jnp.concatenate(done, axis=1)

        done = spread(done, "fsdp", n_near, near_groups)
        done = spread(done, "fsdp", n_wide, wide_groups)
        back = swapped(done, "fsdp", core_pairs)
        blocks = lambda v: [v[:, i * half : (i + 1) * half] for i in range(3)]

        terms = 0.0
        for (_, gate_pre, up_pre), at_row in ((blocks(done), core * half), (blocks(back), (1 - core) * half)):
            for pre, rows in ((gate_pre, gate_rows), (up_pre, up_rows)):
                rows = lax.dynamic_slice_in_dim(rows, at_row, half, 0)
                terms = terms + jnp.dot(pre, rows, preferred_element_type=f32)
        terms = exchange(terms.astype(jnp.bfloat16), "tp")
        input_sum = jnp.sum(terms.reshape(n_tp, -1, width).astype(f32), axis=0).astype(jnp.bfloat16)
        grads = []
        for own, oth, act in zip(blocks(done), blocks(back), (dy_own, x_own, x_own)):
            own = lax.dot_general(own, act, tdims, preferred_element_type=f32)
            oth = lax.dot_general(oth, act, tdims, preferred_element_type=f32)
            grads.append(jnp.where(core == 0, jnp.concatenate([own, oth]), jnp.concatenate([oth, own])))
        down_grad, gate_grad, up_grad = grads
        return (input_sum, gate_grad, up_grad, down_grad)

    spec = P("tp", "fsdp")
    return jax.shard_map(shards, mesh=mesh, in_specs=(spec,) * 5, out_specs=(spec,) * 4, check_vma=False)
```

```python
import jax
import jax.numpy as jnp
from jax import lax
from jax.sharding import PartitionSpec as P

Z_HI, CORES = 4, 2


def activate(gate, up, hidden_grad):
    sig = 1.0 / (1.0 + jnp.exp(-gate))
    hidden = (gate * sig * up).astype(jnp.bfloat16)
    gate_pre = (hidden_grad * up * sig * (1.0 + gate * (1.0 - sig))).astype(jnp.bfloat16)
    up_pre = (hidden_grad * gate * sig).astype(jnp.bfloat16)
    return (hidden, gate_pre, up_pre)


def swapped(value, axis, pairs):
    return lax.ppermute(value, axis, pairs)


def spread(value, axis, count, groups=None):
    copies = jnp.broadcast_to(value[None], (count,) + value.shape).reshape((-1,) + value.shape[1:])
    return exchange(copies, axis, groups)


def exchange(value, axis, groups=None):
    return lax.all_to_all(value, axis, split_axis=0, concat_axis=0, tiled=True, axis_index_groups=groups)


def solution(mesh):
    n_fsdp, n_tp = mesh.shape["fsdp"], mesh.shape["tp"]
    n_x = n_fsdp // (Z_HI * CORES)

    def at(z, x, c):
        return (z * n_x + x) * CORES + c

    zs, xs, cs = range(Z_HI), range(n_x), range(CORES)
    core_pairs = [(at(z, x, c), at(z, x, 1 - c)) for z in zs for x in xs for c in cs]
    far = n_x // 2
    wide_groups = [[at(z, 2 * q + p, 0) for q in range(far)] for z in zs for p in range(2)]
    wide_groups += [[at(z, x, 1) for z in zs] for x in xs]
    near_groups = [[at(z, 2 * q + p, 0) for z in zs for p in range(2)] for q in range(far)]
    near_groups += [[at(z, x, 1) for x in xs] for z in zs]
    n_wide, n_near = len(wide_groups[0]), len(near_groups[0])

    def shards(tokens, out_grad, gate_rows, up_rows, down_rows):
        dims = (((1,), (1,)), ((), ()))
        tdims = (((0,), (0,)), ((), ()))
        f32 = jnp.float32
        width = tokens.shape[1]
        half = gate_rows.shape[0] // CORES
        core = lax.axis_index("fsdp") % CORES

        weights = (gate_rows, up_rows, down_rows)

        def rows_of(which):
            return jnp.concatenate([lax.dynamic_slice_in_dim(w, which * half, half, 0) for w in weights])

        mine, theirs = rows_of(core), rows_of(1 - core)
        got = swapped(theirs, "fsdp", core_pairs)

        copies = [jnp.broadcast_to(v[None], (n_tp,) + v.shape) for v in (tokens, out_grad)]
        group = exchange(jnp.concatenate(copies, axis=2).reshape(-1, 2 * width), "tp")
        group, got = lax.optimization_barrier((group, got))
        other = swapped(group, "fsdp", core_pairs)
        x_own, dy_own = group[:, :width], group[:, width:]

        spans = [slice(i * half, (i + 1) * half) for i in range(3)]
        firsts = [
            lax.dot_general(own, mine[span], dims, preferred_element_type=f32)
            for own, span in zip((x_own, x_own, dy_own), spans)
        ]
        firsts, other = lax.optimization_barrier((firsts, other))
        x_oth, dy_oth = other[:, :width], other[:, width:]
        parts = []
        for first, oth, span in zip(firsts, (x_oth, x_oth, dy_oth), spans):
            part = first + lax.dot_general(oth, got[span], dims, preferred_element_type=f32)
            parts.append(part.astype(jnp.bfloat16))
        pieces = exchange(jnp.concatenate(parts, axis=1), "fsdp", wide_groups)
        sums = jnp.sum(pieces.reshape(n_wide, -1, 3 * half).astype(f32), axis=0).astype(jnp.bfloat16)
        pieces = exchange(sums, "fsdp", near_groups)
        sums = jnp.sum(pieces.reshape(n_near, -1, 3 * half).astype(f32), axis=0)
        done = activate(sums[:, :half], sums[:, half : 2 * half], sums[:, 2 * half :])
        done = jnp.concatenate(done, axis=1)

        done = spread(done, "fsdp", n_near, near_groups)
        done = spread(done, "fsdp", n_wide, wide_groups)
        back = swapped(done, "fsdp", core_pairs)

        terms = jnp.dot(done[:, half:], mine[: 2 * half], preferred_element_type=f32)
        terms = terms + jnp.dot(back[:, half:], theirs[: 2 * half], preferred_element_type=f32)
        terms = exchange(terms.astype(jnp.bfloat16), "tp")
        input_sum = jnp.sum(terms.reshape(n_tp, -1, width).astype(f32), axis=0).astype(jnp.bfloat16)

        def grad(start, act):
            own, oth = [lax.dot_general(v[:, start : start + half], act, tdims, preferred_element_type=f32) for v in (done, back)]
            return jnp.where(core == 0, jnp.concatenate([own, oth]), jnp.concatenate([oth, own]))

        down_grad, gate_grad, up_grad = grad(0, dy_own), grad(half, x_own), grad(2 * half, x_own)
        return (input_sum, gate_grad, up_grad, down_grad)

    spec = P("tp", "fsdp")
    return jax.shard_map(shards, mesh=mesh, in_specs=(spec,) * 5, out_specs=(spec,) * 4, check_vma=False)
```

```python
import jax
import jax.numpy as jnp
from jax import lax
from jax.sharding import PartitionSpec as P

Z_HI, CORES = 4, 2


def activate(gate, up, hidden_grad):
    sig = 1.0 / (1.0 + jnp.exp(-gate))
    hidden = (gate * sig * up).astype(jnp.bfloat16)
    gate_pre = (hidden_grad * up * sig * (1.0 + gate * (1.0 - sig))).astype(jnp.bfloat16)
    up_pre = (hidden_grad * gate * sig).astype(jnp.bfloat16)
    return (hidden, gate_pre, up_pre)


def swapped(value, axis, pairs):
    return lax.ppermute(value, axis, pairs)


def spread(value, axis, count, groups=None):
    copies = jnp.broadcast_to(value[None], (count,) + value.shape).reshape((-1,) + value.shape[1:])
    return exchange(copies, axis, groups)


def exchange(value, axis, groups=None):
    return lax.all_to_all(value, axis, split_axis=0, concat_axis=0, tiled=True, axis_index_groups=groups)


def solution(mesh):
    n_fsdp, n_tp = mesh.shape["fsdp"], mesh.shape["tp"]
    n_x = n_fsdp // (Z_HI * CORES)

    def at(z, x, c):
        return (z * n_x + x) * CORES + c

    zs, xs, cs = range(Z_HI), range(n_x), range(CORES)
    core_pairs = [(at(z, x, c), at(z, x, 1 - c)) for z in zs for x in xs for c in cs]
    far = n_x // 2
    wide_groups = [[at(z, 2 * q + p, 0) for q in range(far)] for z in zs for p in range(2)]
    wide_groups += [[at(z, x, 1) for z in zs] for x in xs]
    near_groups = [[at(z, 2 * q + p, 0) for z in zs for p in range(2)] for q in range(far)]
    near_groups += [[at(z, x, 1) for x in xs] for z in zs]
    n_wide, n_near = len(wide_groups[0]), len(near_groups[0])

    def shards(tokens, out_grad, gate_rows, up_rows, down_rows):
        dims = (((1,), (1,)), ((), ()))
        tdims = (((0,), (0,)), ((), ()))
        f32 = jnp.float32
        width = tokens.shape[1]
        half = gate_rows.shape[0] // CORES
        core = lax.axis_index("fsdp") % CORES

        weights = (gate_rows, up_rows, down_rows)

        def rows_of(which):
            return jnp.concatenate([lax.dynamic_slice_in_dim(w, which * half, half, 0) for w in weights])

        mine, theirs = rows_of(core), rows_of(1 - core)
        got = swapped(theirs, "fsdp", core_pairs)

        group = spread(jnp.concatenate([tokens, out_grad], axis=1), "tp", n_tp)
        group, got = lax.optimization_barrier((group, got))
        other = swapped(group, "fsdp", core_pairs)
        x_own, dy_own = group[:, :width], group[:, width:]

        spans = [slice(i * half, (i + 1) * half) for i in range(3)]
        firsts = [
            lax.dot_general(own, mine[span], dims, preferred_element_type=f32)
            for own, span in zip((x_own, x_own, dy_own), spans)
        ]
        firsts, other = lax.optimization_barrier((firsts, other))
        x_oth, dy_oth = other[:, :width], other[:, width:]
        parts = []
        for first, oth, span in zip(firsts, (x_oth, x_oth, dy_oth), spans):
            part = first + lax.dot_general(oth, got[span], dims, preferred_element_type=f32)
            parts.append(part.astype(jnp.bfloat16))
        pieces = exchange(jnp.concatenate(parts, axis=1), "fsdp", wide_groups)
        sums = jnp.sum(pieces.reshape(n_wide, -1, 3 * half).astype(f32), axis=0).astype(jnp.bfloat16)
        pieces = exchange(sums, "fsdp", near_groups)
        sums = jnp.sum(pieces.reshape(n_near, -1, 3 * half).astype(f32), axis=0)
        done = activate(sums[:, :half], sums[:, half : 2 * half], sums[:, 2 * half :])
        done = jnp.concatenate(done, axis=1)

        done = spread(done, "fsdp", n_near, near_groups)
        done = spread(done, "fsdp", n_wide, wide_groups)

        pre = done[:, half:]
        away = jnp.dot(pre, got[: 2 * half], preferred_element_type=f32).astype(jnp.bfloat16)
        home = jnp.dot(pre, mine[: 2 * half], preferred_element_type=f32)
        came = swapped(away, "fsdp", core_pairs)
        home, came = lax.optimization_barrier((home, came))
        terms = (home + came.astype(f32)).astype(jnp.bfloat16)
        terms, done = lax.optimization_barrier((terms, done))
        terms = exchange(terms, "tp")

        def product(value, i, act):
            return lax.dot_general(value[:, i * half : (i + 1) * half], act, tdims, preferred_element_type=f32)

        acts = (dy_own, x_own, x_own)
        back = swapped(done, "fsdp", core_pairs)
        owns = [product(done, i, acts[i]) for i in range(3)]
        oths = [product(back, i, acts[i]) for i in range(3)]
        down_grad, gate_grad, up_grad = [
            jnp.where(core == 0, jnp.concatenate([own, oth]), jnp.concatenate([oth, own])) for own, oth in zip(owns, oths)
        ]
        terms, down_grad, gate_grad, up_grad = lax.optimization_barrier((terms, down_grad, gate_grad, up_grad))
        input_sum = jnp.sum(terms.reshape(n_tp, -1, width).astype(f32), axis=0).astype(jnp.bfloat16)
        return (input_sum, gate_grad, up_grad, down_grad)

    spec = P("tp", "fsdp")
    return jax.shard_map(shards, mesh=mesh, in_specs=(spec,) * 5, out_specs=(spec,) * 4, check_vma=False)
```

```python
import jax
import jax.numpy as jnp
from jax import lax
from jax.sharding import PartitionSpec as P

Z_HI, CORES = 4, 2


def activate(gate, up, hidden_grad):
    sig = 1.0 / (1.0 + jnp.exp(-gate))
    hidden = (gate * sig * up).astype(jnp.bfloat16)
    gate_pre = (hidden_grad * up * sig * (1.0 + gate * (1.0 - sig))).astype(jnp.bfloat16)
    up_pre = (hidden_grad * gate * sig).astype(jnp.bfloat16)
    return (hidden, gate_pre, up_pre)


def swapped(value, axis, pairs):
    return lax.ppermute(value, axis, pairs)


def spread(value, axis, count, groups=None):
    copies = jnp.broadcast_to(value[None], (count,) + value.shape).reshape((-1,) + value.shape[1:])
    return exchange(copies, axis, groups)


def exchange(value, axis, groups=None):
    return lax.all_to_all(value, axis, split_axis=0, concat_axis=0, tiled=True, axis_index_groups=groups)


def solution(mesh):
    n_fsdp, n_tp = mesh.shape["fsdp"], mesh.shape["tp"]
    n_x = n_fsdp // (Z_HI * CORES)

    def at(z, x, c):
        return (z * n_x + x) * CORES + c

    zs, xs, cs = range(Z_HI), range(n_x), range(CORES)
    core_pairs = [(at(z, x, c), at(z, x, 1 - c)) for z in zs for x in xs for c in cs]
    far = n_x // 2
    wide_groups = [[at(z, 2 * q + p, 0) for q in range(far)] for z in zs for p in range(2)]
    wide_groups += [[at(z, x, 1) for z in zs] for x in xs]
    near_groups = [[at(z, 2 * q + p, 0) for z in zs for p in range(2)] for q in range(far)]
    near_groups += [[at(z, x, 1) for x in xs] for z in zs]
    n_wide, n_near = len(wide_groups[0]), len(near_groups[0])

    def shards(tokens, out_grad, gate_rows, up_rows, down_rows):
        dims = (((1,), (1,)), ((), ()))
        tdims = (((0,), (0,)), ((), ()))
        f32 = jnp.float32
        width = tokens.shape[1]
        half = gate_rows.shape[0] // CORES
        core = lax.axis_index("fsdp") % CORES

        weights = (gate_rows, up_rows, down_rows)

        def rows_of(which):
            return jnp.concatenate([lax.dynamic_slice_in_dim(w, which * half, half, 0) for w in weights])

        mine, theirs = rows_of(core), rows_of(1 - core)
        got = swapped(theirs, "fsdp", core_pairs)

        group = spread(jnp.concatenate([tokens, out_grad], axis=1), "tp", n_tp)
        group, got = lax.optimization_barrier((group, got))
        other = swapped(group, "fsdp", core_pairs)
        x_own, dy_own = group[:, :width], group[:, width:]

        spans = [slice(i * half, (i + 1) * half) for i in range(3)]
        firsts = [
            lax.dot_general(own, mine[span], dims, preferred_element_type=f32)
            for own, span in zip((x_own, x_own, dy_own), spans)
        ]
        firsts, other = lax.optimization_barrier((firsts, other))
        x_oth, dy_oth = other[:, :width], other[:, width:]
        parts = []
        for first, oth, span in zip(firsts, (x_oth, x_oth, dy_oth), spans):
            part = first + lax.dot_general(oth, got[span], dims, preferred_element_type=f32)
            parts.append(part.astype(jnp.bfloat16))
        pieces = exchange(jnp.concatenate(parts, axis=1), "fsdp", wide_groups)
        sums = jnp.sum(pieces.reshape(n_wide, -1, 3 * half).astype(f32), axis=0).astype(jnp.bfloat16)
        pieces = exchange(sums, "fsdp", near_groups)
        sums = jnp.sum(pieces.reshape(n_near, -1, 3 * half).astype(f32), axis=0)
        done = activate(sums[:, :half], sums[:, half : 2 * half], sums[:, 2 * half :])
        done = jnp.concatenate(done, axis=1)

        done = spread(done, "fsdp", n_near, near_groups)
        done = spread(done, "fsdp", n_wide, wide_groups)

        pre = done[:, half:]
        away = jnp.dot(pre, got[: 2 * half], preferred_element_type=f32).astype(jnp.bfloat16)
        home = jnp.dot(pre, mine[: 2 * half], preferred_element_type=f32)

        def product(value, i, act):
            return lax.dot_general(value[:, i * half : (i + 1) * half], act, tdims, preferred_element_type=f32)

        acts = (dy_own, x_own, x_own)
        away, done = lax.optimization_barrier((away, done))
        came = swapped(away, "fsdp", core_pairs)
        owns = [product(done, i, acts[i]) for i in range(3)]
        home, came, owns = lax.optimization_barrier((home, came, owns))
        terms = (home + came.astype(f32)).astype(jnp.bfloat16)
        terms = exchange(terms, "tp")
        back = swapped(done, "fsdp", core_pairs)
        oths = [product(back, i, acts[i]) for i in range(3)]
        down_grad, gate_grad, up_grad = [
            jnp.where(core == 0, jnp.concatenate([own, oth]), jnp.concatenate([oth, own])) for own, oth in zip(owns, oths)
        ]
        terms, down_grad, gate_grad, up_grad = lax.optimization_barrier((terms, down_grad, gate_grad, up_grad))
        input_sum = jnp.sum(terms.reshape(n_tp, -1, width).astype(f32), axis=0).astype(jnp.bfloat16)
        return (input_sum, gate_grad, up_grad, down_grad)

    spec = P("tp", "fsdp")
    return jax.shard_map(shards, mesh=mesh, in_specs=(spec,) * 5, out_specs=(spec,) * 4, check_vma=False)
```

```python
import jax
import jax.numpy as jnp
from jax import lax
from jax.sharding import PartitionSpec as P

Z_HI, CORES = 4, 2


def activate(gate, up, hidden_grad):
    sig = 1.0 / (1.0 + jnp.exp(-gate))
    hidden = (gate * sig * up).astype(jnp.bfloat16)
    gate_pre = (hidden_grad * up * sig * (1.0 + gate * (1.0 - sig))).astype(jnp.bfloat16)
    up_pre = (hidden_grad * gate * sig).astype(jnp.bfloat16)
    return (hidden, gate_pre, up_pre)


def swapped(value, axis, pairs):
    return lax.ppermute(value, axis, pairs)


def spread(value, axis, count, groups=None):
    copies = jnp.broadcast_to(value[None], (count,) + value.shape).reshape((-1,) + value.shape[1:])
    return exchange(copies, axis, groups)


def exchange(value, axis, groups=None):
    return lax.all_to_all(value, axis, split_axis=0, concat_axis=0, tiled=True, axis_index_groups=groups)


def solution(mesh):
    n_fsdp, n_tp = mesh.shape["fsdp"], mesh.shape["tp"]
    n_x = n_fsdp // (Z_HI * CORES)

    def at(z, x, c):
        return (z * n_x + x) * CORES + c

    zs, xs, cs = range(Z_HI), range(n_x), range(CORES)
    core_pairs = [(at(z, x, c), at(z, x, 1 - c)) for z in zs for x in xs for c in cs]
    far = n_x // 2
    wide_groups = [[at(z, 2 * q + p, 0) for q in range(far)] for z in zs for p in range(2)]
    wide_groups += [[at(z, x, 1) for z in zs] for x in xs]
    near_groups = [[at(z, 2 * q + p, 0) for z in zs for p in range(2)] for q in range(far)]
    near_groups += [[at(z, x, 1) for x in xs] for z in zs]
    n_wide, n_near = len(wide_groups[0]), len(near_groups[0])

    def shards(tokens, out_grad, gate_rows, up_rows, down_rows):
        dims = (((1,), (1,)), ((), ()))
        tdims = (((0,), (0,)), ((), ()))
        f32 = jnp.float32
        width = tokens.shape[1]
        half = gate_rows.shape[0] // CORES
        core = lax.axis_index("fsdp") % CORES

        weights = (gate_rows, up_rows, down_rows)

        def rows_of(which):
            return jnp.concatenate([lax.dynamic_slice_in_dim(w, which * half, half, 0) for w in weights])

        mine, theirs = rows_of(core), rows_of(1 - core)
        got = swapped(theirs, "fsdp", core_pairs)

        group = spread(jnp.concatenate([tokens, out_grad], axis=1), "tp", n_tp)
        group, got = lax.optimization_barrier((group, got))
        other = swapped(group, "fsdp", core_pairs)
        x_own, dy_own = group[:, :width], group[:, width:]

        spans = [slice(i * half, (i + 1) * half) for i in range(3)]
        firsts = [
            lax.dot_general(own, mine[span], dims, preferred_element_type=f32)
            for own, span in zip((x_own, x_own, dy_own), spans)
        ]
        firsts, other = lax.optimization_barrier((firsts, other))
        x_oth, dy_oth = other[:, :width], other[:, width:]
        parts = []
        for first, oth, span in zip(firsts, (x_oth, x_oth, dy_oth), spans):
            part = first + lax.dot_general(oth, got[span], dims, preferred_element_type=f32)
            parts.append(part.astype(jnp.bfloat16))
        pieces = exchange(jnp.concatenate(parts, axis=1), "fsdp", wide_groups)
        sums = jnp.sum(pieces.reshape(n_wide, -1, 3 * half).astype(f32), axis=0).astype(jnp.bfloat16)
        pieces = exchange(sums, "fsdp", near_groups)
        sums = jnp.sum(pieces.reshape(n_near, -1, 3 * half).astype(f32), axis=0)
        done = activate(sums[:, :half], sums[:, half : 2 * half], sums[:, 2 * half :])
        done = jnp.concatenate(done, axis=1)

        done = spread(done, "fsdp", n_near, near_groups)
        done = spread(done, "fsdp", n_wide, wide_groups)

        pre = done[:, half:]
        away = jnp.dot(pre, got[: 2 * half], preferred_element_type=f32).astype(jnp.bfloat16)
        home = jnp.dot(pre, mine[: 2 * half], preferred_element_type=f32)
        came = swapped(away, "fsdp", core_pairs)
        terms = (home + came.astype(f32)).astype(jnp.bfloat16)
        terms, done = lax.optimization_barrier((terms, done))
        terms = exchange(terms, "tp")

        def product(value, i, act):
            return lax.dot_general(value[:, i * half : (i + 1) * half], act, tdims, preferred_element_type=f32)

        acts = (dy_own, x_own, x_own)
        back = swapped(done, "fsdp", core_pairs)
        owns = [product(done, i, acts[i]) for i in range(3)]
        oths = [product(back, i, acts[i]) for i in range(3)]
        down_grad, gate_grad, up_grad = [
            jnp.where(core == 0, jnp.concatenate([own, oth]), jnp.concatenate([oth, own])) for own, oth in zip(owns, oths)
        ]
        terms, down_grad, gate_grad, up_grad = lax.optimization_barrier((terms, down_grad, gate_grad, up_grad))
        input_sum = jnp.sum(terms.reshape(n_tp, -1, width).astype(f32), axis=0).astype(jnp.bfloat16)
        return (input_sum, gate_grad, up_grad, down_grad)

    spec = P("tp", "fsdp")
    return jax.shard_map(shards, mesh=mesh, in_specs=(spec,) * 5, out_specs=(spec,) * 4, check_vma=False)
```
